32 devices in a mesh: groups: 2 (over y), row: 4 (over z), col: 4 (over x, core).
Axes of the slice: x: 2, y: 2, z: 4, core: 2. Of those that a mesh axis runs over, the one named last changes fastest.
Arguments:
- features: bfloat16 [8, 2048, 256], P(('groups', 'row'), 'col'), parts along dimension 0, may hold values from -6 to 6
- tile_values: bfloat16 [8, 4, 1024, 4096], P(('groups', 'row'), 'col'), parts along dimension 0, may hold values from -0.125 to 0.125
- tile_rows: int32 [8, 4, 1024], P(('groups', 'row'), 'col'), parts along dimension 0, may hold values from 0 to 31
- tile_cols: int32 [8, 4, 1024], P(('groups', 'row'), 'col'), parts along dimension 0, may hold values from 0 to 31
- counts: int32 [8, 4], P(('groups', 'row'), 'col'), parts along dimension 0, may hold values from 128 to 1024, as said below
- weight: bfloat16 [256, 256], replicated, may hold values from -0.375 to 0.375
- bias: float32 [256], replicated, may hold values from -3 to 3
Outputs:
- layer_out: bfloat16 [8, 2048, 256], P(('groups', 'col'), 'row'), parts along dimension 0
The draws below stay inside these ranges and needn't reach their ends.
There are 2 independent parts, one for each index of `groups`. The reference program is written for one: setup_inputs(seed, part) draws one part's arguments, and reference() takes and returns one part's arrays. A program takes and returns all parts, laid end to end along the dimension named above; an argument that names none is the same for every part. Nothing has to cross between parts.
Inputs may be any that keep to these rules, and one draw needn't show every extreme that they name: Slots at or past counts[r, c] hold values that are to be ignored; coordinate pairs may repeat within a cell, and repeated tiles add. In every draw one grid cell has exactly 1024 live slots.
All inputs are finite; a program needn't handle non-finite values.
Results may differ from the reference program's by a relative error of at most 0.0046.
Values may be sent and summed in bfloat16 or wider, within the bound.
A program may use at most 128 MiB of HBM per device.

```python
import jax
import jax.numpy as jnp
from jax import lax

F = 256
TILE = 64
P_SIZE = 512
TILES = 1024
N_ROW = 4
N_COL = 4


def draw_counts(key, part):
    first_key = jax.random.fold_in(key, 11)
    second_key = jax.random.fold_in(key, 23)
    third_key = jax.random.fold_in(key, 37)
    left_draw = jax.random.randint(first_key, (N_ROW * N_COL,), 1, TILES + 1, dtype=jnp.int32)
    right_draw = jax.random.randint(second_key, (N_ROW * N_COL,), 1, TILES + 1, dtype=jnp.int32)
    loads = jnp.maximum(left_draw * right_draw // TILES, TILES // 8)
    chosen = jax.random.randint(third_key, (), 0, N_ROW * N_COL, dtype=jnp.int32)
    loads = loads.at[chosen].set(TILES)
    return loads.reshape(N_ROW, N_COL).astype(jnp.int32)


def touch_ends(array, key, low, top_value):
    longest = array.shape.index(max(array.shape))
    spots = []
    for shift in (0, 1):
        where = [jax.random.randint(jax.random.fold_in(key, axis), (), 0, length) for axis, length in enumerate(array.shape)]
        where[longest] = (where[longest] + shift) % array.shape[longest]
        spots.append(tuple(where))
    return array.at[spots[0]].set(low).at[spots[1]].set(top_value)


def level_of(own_key, extent, split, least, high):
    def one(axis_at, blocks):
        heights = jax.random.uniform(jax.random.fold_in(jax.random.fold_in(own_key, 6), axis_at), (blocks,), jnp.float32, least / len(split), high / len(split))
        return jnp.repeat(jnp.exp(heights), extent[axis_at] // blocks).reshape((-1,) + (1,) * (len(extent) - axis_at - 1))

    gain = one(*split[0])
    for cut in split[1:]:
        gain = gain * one(*cut)
    return gain


def scatter_about(stream_key, shape, width, bound, shards=(), held_as=jnp.bfloat16):
    gain = level_of(stream_key, shape, shards, -0.22, 0.18) if shards else 1.0
    entries = jax.random.normal(stream_key, shape, jnp.float32) * width * gain
    return jnp.minimum(jnp.maximum(entries, -bound), bound).astype(held_as)


def setup_inputs(seed: int = 0, part: int = 0) -> dict:
    key_list = jax.random.split(jax.random.key(seed), 8)
    own_keys = jax.random.split(jax.random.fold_in(key_list[7], part), 8)
    return {
        "features": scatter_about(own_keys[0], (N_ROW, N_COL * P_SIZE, F), 1.0, 6.0, ((0, 4), (1, 4))),
        "tile_values": scatter_about(own_keys[1], (N_ROW, N_COL, TILES, TILE * TILE), (TILES * TILE * TILE // (4 * P_SIZE)) ** -0.5, 0.125, ((0, 4), (1, 4))),
        "tile_rows": touch_ends(jax.random.randint(own_keys[2], (N_ROW, N_COL, TILES), 0, N_ROW * P_SIZE // TILE), jax.random.fold_in(own_keys[2], 1), 0, (N_ROW * P_SIZE // TILE) - 1).astype(jnp.int32),
        "tile_cols": touch_ends(jax.random.randint(own_keys[3], (N_ROW, N_COL, TILES), 0, N_COL * P_SIZE // TILE), jax.random.fold_in(own_keys[3], 1), 0, (N_COL * P_SIZE // TILE) - 1).astype(jnp.int32),
        "counts": draw_counts(jax.random.fold_in(jax.random.fold_in(key_list[7], part), 71), part),
        "weight": scatter_about(key_list[5], (F, F), F ** -0.5, 0.375),
        "bias": scatter_about(key_list[6], (F,), 0.5, 3.0, (), jnp.float32),
    }


def reference(features, tile_values, tile_rows, tile_cols, counts, weight, bias):
    block_size = min(128, TILES)
    out_tiles = N_ROW * P_SIZE // TILE
    running = jnp.zeros((N_COL, out_tiles, TILE, F), jnp.float32)
    cells = N_ROW * N_COL
    all_values = tile_values.reshape(cells, TILES, TILE * TILE)
    all_rows = tile_rows.reshape(cells, TILES).astype(jnp.int32)
    all_cols = tile_cols.reshape(cells, TILES).astype(jnp.int32)
    all_counts = counts.reshape(cells).astype(jnp.int32)
    cell_index = jnp.arange(cells, dtype=jnp.int32)
    grid_rows = cell_index // N_COL
    grid_cols = cell_index % N_COL

    def cell_step(running, item):
        values, tile_row, tile_col, live_count, grid_row, grid_col = item
        source = lax.dynamic_index_in_dim(features, grid_row, 0, keepdims=False).reshape(N_COL * P_SIZE // TILE, TILE, F)

        def block_step(block_index, running):
            first_slot = (block_index * block_size).astype(jnp.int32)
            tile_block = lax.dynamic_slice_in_dim(values, first_slot, block_size, 0).reshape(block_size, TILE, TILE).astype(jnp.float32)
            target_rows = lax.dynamic_slice_in_dim(tile_row, first_slot, block_size, 0)
            source_cols = lax.dynamic_slice_in_dim(tile_col, first_slot, block_size, 0)
            inputs = source[source_cols].astype(jnp.float32)
            products = jnp.einsum('bij,bjf->bif', tile_block, inputs, precision=lax.Precision.HIGHEST)
            is_live = first_slot + jnp.arange(block_size, dtype=jnp.int32) < live_count
            target = jnp.where(is_live, target_rows, out_tiles)
            return running.at[grid_col, target].add(products, mode="drop")

        block_count = (live_count + block_size - 1) // block_size
        running = lax.fori_loop(0, block_count, block_step, running)
        return running, None

    running, unused = lax.scan(cell_step, running, (all_values, all_rows, all_cols, all_counts, grid_rows, grid_cols))
    hidden = running.reshape(N_COL * N_ROW * P_SIZE, F).astype(jnp.bfloat16)
    mixed = jnp.dot(hidden, weight, preferred_element_type=jnp.float32) + bias.astype(jnp.float32)
    return jnp.maximum(mixed, 0.0).astype(jnp.bfloat16).reshape(N_COL, N_ROW * P_SIZE, F)
```

```python
import functools

import jax
import jax.numpy as jnp
from jax import lax
from jax.experimental import pallas as pl
from jax.experimental.pallas import tpu as pltpu
from jax.sharding import PartitionSpec as P

TILE = 64
LANES = 128


def partial_kernel(
    n_row, live_ref, vals_ref, rows_ref, cols_ref, src_ref, out_ref, pick, dense, swapped
):
    tiles_in, slots = pick.shape
    lanes = vals_ref.shape[-1]
    col_tiles = src_ref.shape[0] // TILE
    row_tiles = tiles_in // col_tiles
    half = tiles_in // 2
    chunk = min(half, 512)
    pairs = chunk // row_tiles

    @pl.when(pl.program_id(0) == 0)
    def _():
        row = rows_ref[0]
        col = cols_ref[0]
        slot = lax.broadcasted_iota(jnp.int32, (1, slots), 1)
        place = (col & 1) * half + (col >> 1) * row_tiles + row
        place = jnp.where(slot < live_ref[0, 0], place, -1)

        @pl.loop(0, tiles_in // 128)
        def _(at):
            first = pl.multiple_of(at * 128, 128)
            index = first + lax.broadcasted_iota(jnp.int32, (128, slots), 0)
            pick[pl.ds(first, 128), :] = jnp.where(index == place, 1.0, 0.0).astype(
                jnp.bfloat16
            )

        for pair in range(col_tiles // 2):
            low = 2 * pair * TILE
            swapped[low : low + TILE, :] = src_ref[low + TILE : low + 2 * TILE, :]
            swapped[low + TILE : low + 2 * TILE, :] = src_ref[low : low + TILE, :]

    is_low = lax.broadcasted_iota(jnp.int32, (row_tiles, LANES), 1) < TILE

    def one_chunk(at, carry):
        first = pl.multiple_of(at * chunk, chunk)
        for sub in range(lanes // 256):
            vals = vals_ref[0, 0, :, sub * 256 : (sub + 1) * 256]
            even = jnp.dot(
                pick[pl.ds(first, chunk), :], vals, preferred_element_type=jnp.float32
            )
            odd = jnp.dot(
                pick[pl.ds(half + first, chunk), :],
                vals,
                preferred_element_type=jnp.float32,
            )
            for part in range(2):
                block = 2 * sub + part
                for pair in range(pairs):
                    held = even[
                        pair * row_tiles : (pair + 1) * row_tiles,
                        part * LANES : (part + 1) * LANES,
                    ]
                    turned = pltpu.roll(
                        odd[
                            pair * row_tiles : (pair + 1) * row_tiles,
                            part * LANES : (part + 1) * LANES,
                        ],
                        TILE,
                        1,
                    )
                    lane = pl.multiple_of((at * pairs + pair) * LANES, LANES)
                    where = pl.ds(block * row_tiles, row_tiles), pl.ds(lane, LANES)
                    dense[(0,) + where] = jnp.where(is_low, held, turned).astype(
                        jnp.bfloat16
                    )
                    dense[(1,) + where] = jnp.where(is_low, turned, held).astype(
                        jnp.bfloat16
                    )
        return carry

    if half == chunk:
        one_chunk(0, 0)
    else:
        lax.fori_loop(0, half // chunk, one_chunk, 0)

    own = row_tiles // n_row
    for parity, source in ((0, src_ref), (1, swapped)):
        sums = jnp.dot(
            dense[parity], source[...], preferred_element_type=jnp.float32
        )
        for block in range(lanes // LANES):
            for owner in range(n_row):
                low = block * row_tiles + owner * own
                out_ref[owner, 2 * block + parity] = sums[low : low + own, :]


def partial_sums(n_row, live, vals, rows, cols, source):
    slots = vals.shape[2]
    width = source.shape[1]
    row_tiles = n_row * 8
    col_tiles = source.shape[0] // TILE
    tiles_in = row_tiles * col_tiles
    lanes = 1024
    blocks = lanes // LANES
    return pl.pallas_call(
        functools.partial(partial_kernel, n_row),
        grid=(vals.shape[3] // lanes,),
        in_specs=[
            pl.BlockSpec(memory_space=pltpu.SMEM),
            pl.BlockSpec((1, 1, slots, lanes), lambda k: (0, 0, 0, k)),
            pl.BlockSpec((1, 1, slots), lambda k: (0, 0, 0)),
            pl.BlockSpec((1, 1, slots), lambda k: (0, 0, 0)),
            pl.BlockSpec(source.shape, lambda k: (0, 0)),
        ],
        out_specs=pl.BlockSpec((n_row, 2 * blocks, 8, width), lambda k: (0, k, 0, 0)),
        out_shape=jax.ShapeDtypeStruct((n_row, TILE, 8, width), jnp.float32),
        scratch_shapes=[
            pltpu.VMEM((tiles_in, slots), jnp.bfloat16),
            pltpu.VMEM((2, blocks * row_tiles, source.shape[0] ), jnp.bfloat16),
            pltpu.VMEM(source.shape, jnp.bfloat16),
        ],
        compiler_params=pltpu.CompilerParams(vmem_limit_bytes=60 * 1024 * 1024),
    )(live, vals, rows, cols, source)


def on_device(features, tile_values, tile_rows, tile_cols, counts, weight, bias):
    piece_rows = features.shape[1]
    feat_width = features.shape[2]
    n_row = lax.axis_size("row")
    gathered = lax.all_gather(features, "col", axis=1, tiled=True)
    source = gathered.reshape(-1, feat_width)
    sums = partial_sums(n_row, counts, tile_values, tile_rows, tile_cols, source)
    own_rows = lax.psum_scatter(sums, "row", scatter_dimension=0, tiled=True)
    hidden = own_rows[0].astype(jnp.bfloat16).transpose(1, 0, 2).reshape(-1, feat_width)
    mixed = jnp.dot(hidden, weight, preferred_element_type=jnp.float32) + bias
    return jnp.maximum(mixed, 0.0).astype(jnp.bfloat16).reshape(1, piece_rows, feat_width)


def solution(mesh):
    in_specs = (
        P(("groups", "row"), "col", None),
        P(("groups", "row"), "col", None, None),
        P(("groups", "row"), "col", None),
        P(("groups", "row"), "col", None),
        P(("groups", "row"), "col"),
        P(),
        P(),
    )
    out_specs = P(("groups", "col"), "row", None)
    return jax.shard_map(
        on_device, mesh=mesh, in_specs=in_specs, out_specs=out_specs, check_vma=False
    )
```

```python
import functools

import jax
import jax.numpy as jnp
from jax import lax
from jax.experimental import pallas as pl
from jax.experimental.pallas import tpu as pltpu
from jax.sharding import PartitionSpec as P

TILE = 64
LANES = 128
MESH = pl.DeviceIdType.MESH


def layer_kernel(
    n_row, n_col, live_ref, vals_hbm, rows_ref, cols_ref, feat_ref, weight_ref, bias_ref,
    out_ref, vals, pick, dense, src, swapped, acc, sent, up_in, down_in,
    vals_sem, far_send, far_recv, near_send, near_recv, send_sem, up_sem, down_sem,
):
    steps, slots, lanes = vals.shape
    tiles_in = pick.shape[0]
    piece_rows = feat_ref.shape[1]
    col_tiles = src.shape[0] // TILE
    row_tiles = tiles_in // col_tiles
    half = tiles_in // 2
    chunk = min(half, 512)
    pairs = chunk // row_tiles
    own = row_tiles // n_row
    blocks = lanes // LANES
    chips = n_col // 2
    z = lax.axis_index("row")
    me = lax.axis_index("col")
    core = lax.rem(me, 2)
    sibling = me + 1 - 2 * core

    def load(step):
        return pltpu.make_async_copy(
            vals_hbm.at[0, 0, :, pl.ds(pl.multiple_of(step * lanes, lanes), lanes)],
            vals.at[step], vals_sem.at[step],
        )

    for step in range(steps):
        load(step).start()

    def rows_of(index):
        return src.at[pl.ds(pl.multiple_of(index * piece_rows, piece_rows), piece_rows)]

    def far(d):
        return pltpu.make_async_remote_copy(
            src_ref=feat_ref.at[0], dst_ref=rows_of(me),
            send_sem=far_send.at[d], recv_sem=far_recv.at[d],
            device_id={"col": lax.rem(me + 2 * d, n_col)}, device_id_type=MESH,
        )

    def near(d):
        origin = lax.rem(me + n_col - 2 * d, n_col)
        return pltpu.make_async_remote_copy(
            src_ref=feat_ref.at[0] if d == 0 else rows_of(origin), dst_ref=rows_of(origin),
            send_sem=near_send.at[d], recv_sem=near_recv.at[d],
            device_id={"col": sibling}, device_id_type=MESH,
        )

    def passed(p, o, to, sem):
        landing = up_in if sem is up_sem else down_in
        return pltpu.make_async_remote_copy(
            src_ref=sent.at[p, o], dst_ref=landing.at[p, o],
            send_sem=send_sem.at[p, o], recv_sem=sem.at[p, o],
            device_id={"row": to}, device_id_type=MESH,
        )

    barrier = pltpu.get_barrier_semaphore()
    for d in range(1, chips):
        pl.semaphore_signal(
            barrier, inc=1, device_id={"col": lax.rem(me + 2 * d, n_col)}, device_id_type=MESH
        )
    pl.semaphore_signal(barrier, inc=1, device_id={"col": sibling}, device_id_type=MESH)

    @pl.when(z > 0)
    def _():
        pl.semaphore_signal(barrier, inc=1, device_id={"row": z - 1}, device_id_type=MESH)

    @pl.when(z < n_row - 1)
    def _():
        pl.semaphore_signal(barrier, inc=1, device_id={"row": z + 1}, device_id_type=MESH)

    beside = lax.div(z + n_row - 1, n_row) + lax.div(2 * n_row - 2 - z, n_row)
    pl.semaphore_wait(barrier, chips + beside)

    for d in range(1, chips):
        far(d).start()
    near(0).start()
    rows_of(me)[...] = feat_ref[0]

    slot = lax.broadcasted_iota(jnp.int32, (1, slots), 1)
    place = (cols_ref[0] & 1) * half + (cols_ref[0] >> 1) * row_tiles + rows_ref[0]
    place = jnp.where(slot < live_ref[0, 0], place, -1)

    @pl.loop(0, tiles_in // 128)
    def _(at):
        first = pl.multiple_of(at * 128, 128)
        index = first + lax.broadcasted_iota(jnp.int32, (128, slots), 0)
        pick[pl.ds(first, 128), :] = jnp.where(index == place, 1.0, 0.0).astype(jnp.bfloat16)

    is_low = lax.broadcasted_iota(jnp.int32, (row_tiles, LANES), 1) < TILE

    def densify(step):
        def one_chunk(at, carry):
            first = pl.multiple_of(at * chunk, chunk)
            for sub in range(lanes // 256):
                block_vals = vals[step, :, sub * 256 : (sub + 1) * 256]
                even = jnp.dot(
                    pick[pl.ds(first, chunk), :], block_vals,
                    preferred_element_type=jnp.float32,
                )
                odd = jnp.dot(
                    pick[pl.ds(half + first, chunk), :], block_vals,
                    preferred_element_type=jnp.float32,
                )
                for part in range(2):
                    block = 2 * sub + part
                    cut = slice(part * LANES, (part + 1) * LANES)
                    for pair in range(pairs):
                        down = slice(pair * row_tiles, (pair + 1) * row_tiles)
                        held = even[down, cut]
                        turned = pltpu.roll(odd[down, cut], TILE, 1)
                        lane = pl.multiple_of((at * pairs + pair) * LANES, LANES)
                        where = pl.ds(block * row_tiles, row_tiles), pl.ds(lane, LANES)
                        dense[(0,) + where] = jnp.where(is_low, held, turned).astype(jnp.bfloat16)
                        dense[(1,) + where] = jnp.where(is_low, turned, held).astype(jnp.bfloat16)
            return carry

        if half == chunk:
            one_chunk(0, 0)
        else:
            lax.fori_loop(0, half // chunk, one_chunk, 0)

    def finish_gather():
        for d in range(1, chips):
            far(d).wait_recv()
            near(d).start()
        for d in range(chips):
            near(d).wait_recv()
        for pair in range(col_tiles // 2):
            low = 2 * pair * TILE
            swapped[low : low + TILE, :] = src[low + TILE : low + 2 * TILE, :]
            swapped[low + TILE : low + 2 * TILE, :] = src[low : low + TILE, :]

    def multiply(step):
        for parity, source in ((0, src), (1, swapped)):
            sums = jnp.dot(dense[parity], source[...], preferred_element_type=jnp.float32)
            for block in range(blocks):
                for owner in range(n_row):
                    low = block * row_tiles + owner * own
                    to = (2 * block + parity) * own
                    acc[step, owner, to : to + own, :] = sums[low : low + own, :]

    def pass_on(p, is_first, sem, landing, to, owner_of, count):
        def one(j, carry):
            o = owner_of(j)

            @pl.when(is_first)
            def _():
                sent[p, o] = acc[p, o].astype(jnp.bfloat16)

            @pl.when(jnp.logical_not(is_first))
            def _():
                passed(p, o, to, sem).wait_recv()
                sent[p, o] = (acc[p, o] + landing[p, o].astype(jnp.float32)).astype(jnp.bfloat16)

            passed(p, o, to, sem).start()
            return carry

        lax.fori_loop(0, count, one, 0)

        @pl.when(jnp.logical_not(is_first))
        def _():
            passed(p, z, to, sem).wait_recv()
            acc[p, z] = acc[p, z] + landing[p, z].astype(jnp.float32)

    def one_step(t, carry):
        @pl.when(t < steps)
        def _():
            load(t).wait()
            densify(t)

            @pl.when(t == 0)
            def _():
                finish_gather()

            multiply(t)

        up = t - z

        @pl.when(jnp.logical_and(up >= 0, up < steps))
        def _():
            pass_on(up, z == 0, up_sem, up_in, z + 1, lambda j: n_row - 1 - j, n_row - 1 - z)

        below = t - (n_row - 1 - z)

        @pl.when(jnp.logical_and(below >= 0, below < steps))
        def _():
            pass_on(below, z == n_row - 1, down_sem, down_in, z - 1, lambda j: j, z)

        return carry

    lax.fori_loop(0, steps + n_row - 1, one_step, 0)

    hidden = jnp.concatenate([acc[p, z].astype(jnp.bfloat16) for p in range(steps)], axis=0)
    target = lax.broadcasted_iota(jnp.int32, (piece_rows, piece_rows), 0)
    origin = lax.broadcasted_iota(jnp.int32, (piece_rows, piece_rows), 1)
    wanted = (target & (TILE - 1)) * own + (target >> 6)
    order = jnp.where(origin == wanted, 1.0, 0.0).astype(jnp.bfloat16)
    hidden = jnp.dot(order, hidden, preferred_element_type=jnp.float32).astype(jnp.bfloat16)
    mixed = jnp.dot(hidden, weight_ref[...], preferred_element_type=jnp.float32) + bias_ref[...]
    out_ref[0] = jnp.maximum(mixed, 0.0).astype(jnp.bfloat16)

    for d in range(1, chips):
        far(d).wait_send()
    for d in range(chips):
        near(d).wait_send()

    def drain(p, carry):
        def up_one(o, inner):
            passed(p, o, z + 1, up_sem).wait_send()
            return inner

        def down_one(o, inner):
            passed(p, o, z - 1, down_sem).wait_send()
            return inner

        lax.fori_loop(z + 1, n_row, up_one, 0)
        lax.fori_loop(0, z, down_one, 0)
        return carry

    lax.fori_loop(0, steps, drain, 0)


def on_device(features, tile_values, tile_rows, tile_cols, counts, weight, bias):
    n_row, n_col = lax.axis_size("row"), lax.axis_size("col")
    piece_rows, width = features.shape[1:]
    slots, entries = tile_values.shape[2:]
    own = piece_rows // TILE
    row_tiles = n_row * own
    source_rows = n_col * piece_rows
    tiles_in = row_tiles * source_rows // TILE
    steps = 4 if tiles_in <= 2048 else 8
    lanes = entries // steps
    blocks = lanes // LANES
    part_rows = 2 * blocks * own
    vmem = pl.BlockSpec(memory_space=pltpu.VMEM)
    slabs = (steps, n_row, part_rows, width)
    dma = pltpu.SemaphoreType.DMA
    return pl.pallas_call(
        functools.partial(layer_kernel, n_row, n_col),
        in_specs=[
            pl.BlockSpec(memory_space=pltpu.SMEM), pl.BlockSpec(memory_space=pl.ANY),
            vmem, vmem, vmem, vmem, vmem,
        ],
        out_specs=vmem,
        out_shape=jax.ShapeDtypeStruct((1, piece_rows, width), jnp.bfloat16),
        scratch_shapes=[
            pltpu.VMEM((steps, slots, lanes), jnp.bfloat16),
            pltpu.VMEM((tiles_in, slots), jnp.bfloat16),
            pltpu.VMEM((2, blocks * row_tiles, source_rows), jnp.bfloat16),
            pltpu.VMEM((source_rows, width), jnp.bfloat16),
            pltpu.VMEM((source_rows, width), jnp.bfloat16),
            pltpu.VMEM(slabs, jnp.float32),
            pltpu.VMEM(slabs, jnp.bfloat16),
            pltpu.VMEM(slabs, jnp.bfloat16),
            pltpu.VMEM(slabs, jnp.bfloat16),
            dma((steps,)), dma((n_col // 2,)), dma((n_col // 2,)),
            dma((n_col // 2,)), dma((n_col // 2,)),
            dma((steps, n_row)), dma((steps, n_row)), dma((steps, n_row)),
        ],
        compiler_params=pltpu.CompilerParams(
            collective_id=0, has_side_effects=True, vmem_limit_bytes=62 * 1024 * 1024
        ),
    )(counts, tile_values, tile_rows, tile_cols, features, weight, bias.reshape(1, width))


def solution(mesh):
    in_specs = (
        P(("groups", "row"), "col", None),
        P(("groups", "row"), "col", None, None),
        P(("groups", "row"), "col", None),
        P(("groups", "row"), "col", None),
        P(("groups", "row"), "col"),
        P(),
        P(),
    )
    out_specs = P(("groups", "col"), "row", None)
    return jax.shard_map(
        on_device, mesh=mesh, in_specs=in_specs, out_specs=out_specs, check_vma=False
    )
```

```python
import functools

import jax
import jax.numpy as jnp
from jax import lax
from jax.experimental import pallas as pl
from jax.experimental.pallas import tpu as pltpu
from jax.sharding import PartitionSpec as P

TILE = 64
LANES = 128
MESH = pl.DeviceIdType.MESH


def layer_kernel(
    n_row, n_col, live_ref, vals_hbm, rows_ref, cols_ref, feat_ref, weight_ref, bias_ref,
    out_ref, vals, pick, dense, src, swapped, acc, sent, up_in, down_in,
    vals_sem, far_send, far_recv, near_send, near_recv, send_sem, up_sem, down_sem,
):
    steps, slots, lanes = vals.shape
    tiles_in = pick.shape[0]
    piece_rows = feat_ref.shape[1]
    col_tiles = src.shape[0] // TILE
    row_tiles = tiles_in // col_tiles
    half = tiles_in // 2
    chunk = min(half, 512)
    pairs = chunk // row_tiles
    own = row_tiles // n_row
    blocks = lanes // LANES
    chips = n_col // 2
    z = lax.axis_index("row")
    me = lax.axis_index("col")
    core = lax.rem(me, 2)
    sibling = me + 1 - 2 * core

    def load(step):
        return pltpu.make_async_copy(
            vals_hbm.at[0, 0, :, pl.ds(pl.multiple_of(step * lanes, lanes), lanes)],
            vals.at[step], vals_sem.at[step],
        )

    for step in range(steps):
        load(step).start()

    def rows_of(index):
        return src.at[pl.ds(pl.multiple_of(index * piece_rows, piece_rows), piece_rows)]

    def far(d):
        return pltpu.make_async_remote_copy(
            src_ref=feat_ref.at[0], dst_ref=rows_of(me),
            send_sem=far_send.at[d], recv_sem=far_recv.at[d],
            device_id={"col": lax.rem(me + 2 * d, n_col)}, device_id_type=MESH,
        )

    def near(d):
        origin = lax.rem(me + n_col - 2 * d, n_col)
        return pltpu.make_async_remote_copy(
            src_ref=feat_ref.at[0] if d == 0 else rows_of(origin), dst_ref=rows_of(origin),
            send_sem=near_send.at[d], recv_sem=near_recv.at[d],
            device_id={"col": sibling}, device_id_type=MESH,
        )

    def passed(p, o, to, sem):
        landing = up_in if sem is up_sem else down_in
        return pltpu.make_async_remote_copy(
            src_ref=sent.at[p, o], dst_ref=landing.at[p, o],
            send_sem=send_sem.at[p, o], recv_sem=sem.at[p, o],
            device_id={"row": to}, device_id_type=MESH,
        )

    barrier = pltpu.get_barrier_semaphore()
    for d in range(1, chips):
        pl.semaphore_signal(
            barrier, inc=1, device_id={"col": lax.rem(me + 2 * d, n_col)}, device_id_type=MESH
        )
    pl.semaphore_signal(barrier, inc=1, device_id={"col": sibling}, device_id_type=MESH)

    @pl.when(z > 0)
    def _():
        pl.semaphore_signal(barrier, inc=1, device_id={"row": z - 1}, device_id_type=MESH)

    @pl.when(z < n_row - 1)
    def _():
        pl.semaphore_signal(barrier, inc=1, device_id={"row": z + 1}, device_id_type=MESH)

    beside = lax.div(z + n_row - 1, n_row) + lax.div(2 * n_row - 2 - z, n_row)
    pl.semaphore_wait(barrier, chips + beside)

    for d in range(1, chips):
        far(d).start()
    near(0).start()
    rows_of(me)[...] = feat_ref[0]

    slot = lax.broadcasted_iota(jnp.int32, (1, slots), 1)
    place = (cols_ref[0] & 1) * half + (cols_ref[0] >> 1) * row_tiles + rows_ref[0]
    place = jnp.where(slot < live_ref[0, 0], place, -1)

    @pl.loop(0, tiles_in // 128)
    def _(at):
        first = pl.multiple_of(at * 128, 128)
        index = first + lax.broadcasted_iota(jnp.int32, (128, slots), 0)
        pick[pl.ds(first, 128), :] = jnp.where(index == place, 1.0, 0.0).astype(jnp.bfloat16)

    is_low = lax.broadcasted_iota(jnp.int32, (row_tiles, LANES), 1) < TILE

    def densify(step):
        def one_chunk(at, carry):
            first = pl.multiple_of(at * chunk, chunk)
            for sub in range(lanes // 256):
                block_vals = vals[step, :, sub * 256 : (sub + 1) * 256]
                even = jnp.dot(
                    pick[pl.ds(first, chunk), :], block_vals,
                    preferred_element_type=jnp.float32,
                )
                odd = jnp.dot(
                    pick[pl.ds(half + first, chunk), :], block_vals,
                    preferred_element_type=jnp.float32,
                )
                for part in range(2):
                    block = 2 * sub + part
                    cut = slice(part * LANES, (part + 1) * LANES)
                    for pair in range(pairs):
                        down = slice(pair * row_tiles, (pair + 1) * row_tiles)
                        held = even[down, cut]
                        turned = pltpu.roll(odd[down, cut], TILE, 1)
                        lane = pl.multiple_of((at * pairs + pair) * LANES, LANES)
                        where = pl.ds(block * row_tiles, row_tiles), pl.ds(lane, LANES)
                        dense[(0,) + where] = jnp.where(is_low, held, turned).astype(jnp.bfloat16)
                        dense[(1,) + where] = jnp.where(is_low, turned, held).astype(jnp.bfloat16)
            return carry

        if half == chunk:
            one_chunk(0, 0)
        else:
            lax.fori_loop(0, half // chunk, one_chunk, 0)

    def finish_gather():
        for d in range(1, chips):
            far(d).wait_recv()
            near(d).start()
        for d in range(chips):
            near(d).wait_recv()
        for pair in range(col_tiles // 2):
            low = 2 * pair * TILE
            swapped[low : low + TILE, :] = src[low + TILE : low + 2 * TILE, :]
            swapped[low + TILE : low + 2 * TILE, :] = src[low : low + TILE, :]

    def multiply(step):
        for parity, source in ((0, src), (1, swapped)):
            sums = jnp.dot(dense[parity], source[...], preferred_element_type=jnp.float32)
            for block in range(blocks):
                for owner in range(n_row):
                    low = block * row_tiles + owner * own
                    to = (2 * block + parity) * own
                    acc[step, owner, to : to + own, :] = sums[low : low + own, :]

    def pass_on(p, is_first, sem, landing, to, owner_of, begin, end):
        def one(j, carry):
            o = owner_of(j)

            @pl.when(is_first)
            def _():
                sent[p, o] = acc[p, o].astype(jnp.bfloat16)

            @pl.when(jnp.logical_not(is_first))
            def _():
                passed(p, o, to, sem).wait_recv()
                sent[p, o] = (acc[p, o] + landing[p, o].astype(jnp.float32)).astype(jnp.bfloat16)

            passed(p, o, to, sem).start()
            return carry

        lax.fori_loop(begin, end, one, 0)

    above_count = n_row - 1 - z
    below_count = z
    above_early = jnp.minimum(above_count, jnp.maximum(above_count - 1, 1))
    below_early = jnp.minimum(below_count, jnp.maximum(below_count - 1, 1))

    def pass_up(p, begin, end):
        pass_on(p, z == 0, up_sem, up_in, z + 1, lambda j: n_row - 1 - j, begin, end)

    def pass_down(p, begin, end):
        pass_on(p, z == n_row - 1, down_sem, down_in, z - 1, lambda j: j, begin, end)

    def one_step(t, carry):
        @pl.when(t < steps)
        def _():
            load(t).wait()
            densify(t)

            @pl.when(t == 0)
            def _():
                finish_gather()

            multiply(t)

        up = t - z

        @pl.when(jnp.logical_and(up >= 0, up < steps))
        def _():
            pass_up(up, 0, above_early)

        below = t - (n_row - 1 - z)

        @pl.when(jnp.logical_and(below >= 0, below < steps))
        def _():
            pass_down(below, 0, below_early)

        return carry

    lax.fori_loop(0, steps + n_row - 1, one_step, 0)

    def late(p, carry):
        pass_up(p, above_early, above_count)
        pass_down(p, below_early, below_count)
        return carry

    lax.fori_loop(0, steps, late, 0)

    def collect(p, carry):
        @pl.when(z > 0)
        def _():
            passed(p, z, z + 1, up_sem).wait_recv()
            acc[p, z] = acc[p, z] + up_in[p, z].astype(jnp.float32)

        @pl.when(z < n_row - 1)
        def _():
            passed(p, z, z - 1, down_sem).wait_recv()
            acc[p, z] = acc[p, z] + down_in[p, z].astype(jnp.float32)

        return carry

    lax.fori_loop(0, steps, collect, 0)

    hidden = jnp.concatenate([acc[p, z].astype(jnp.bfloat16) for p in range(steps)], axis=0)
    target = lax.broadcasted_iota(jnp.int32, (piece_rows, piece_rows), 0)
    origin = lax.broadcasted_iota(jnp.int32, (piece_rows, piece_rows), 1)
    wanted = (target & (TILE - 1)) * own + (target >> 6)
    order = jnp.where(origin == wanted, 1.0, 0.0).astype(jnp.bfloat16)
    hidden = jnp.dot(order, hidden, preferred_element_type=jnp.float32).astype(jnp.bfloat16)
    mixed = jnp.dot(hidden, weight_ref[...], preferred_element_type=jnp.float32) + bias_ref[...]
    out_ref[0] = jnp.maximum(mixed, 0.0).astype(jnp.bfloat16)

    for d in range(1, chips):
        far(d).wait_send()
    for d in range(chips):
        near(d).wait_send()

    def drain(p, carry):
        def up_one(o, inner):
            passed(p, o, z + 1, up_sem).wait_send()
            return inner

        def down_one(o, inner):
            passed(p, o, z - 1, down_sem).wait_send()
            return inner

        lax.fori_loop(z + 1, n_row, up_one, 0)
        lax.fori_loop(0, z, down_one, 0)
        return carry

    lax.fori_loop(0, steps, drain, 0)


def on_device(features, tile_values, tile_rows, tile_cols, counts, weight, bias):
    n_row, n_col = lax.axis_size("row"), lax.axis_size("col")
    piece_rows, width = features.shape[1:]
    slots, entries = tile_values.shape[2:]
    own = piece_rows // TILE
    row_tiles = n_row * own
    source_rows = n_col * piece_rows
    tiles_in = row_tiles * source_rows // TILE
    steps = 4 if tiles_in <= 2048 else 8
    lanes = entries // steps
    blocks = lanes // LANES
    part_rows = 2 * blocks * own
    vmem = pl.BlockSpec(memory_space=pltpu.VMEM)
    slabs = (steps, n_row, part_rows, width)
    dma = pltpu.SemaphoreType.DMA
    return pl.pallas_call(
        functools.partial(layer_kernel, n_row, n_col),
        in_specs=[
            pl.BlockSpec(memory_space=pltpu.SMEM), pl.BlockSpec(memory_space=pl.ANY),
            vmem, vmem, vmem, vmem, vmem,
        ],
        out_specs=vmem,
        out_shape=jax.ShapeDtypeStruct((1, piece_rows, width), jnp.bfloat16),
        scratch_shapes=[
            pltpu.VMEM((steps, slots, lanes), jnp.bfloat16),
            pltpu.VMEM((tiles_in, slots), jnp.bfloat16),
            pltpu.VMEM((2, blocks * row_tiles, source_rows), jnp.bfloat16),
            pltpu.VMEM((source_rows, width), jnp.bfloat16),
            pltpu.VMEM((source_rows, width), jnp.bfloat16),
            pltpu.VMEM(slabs, jnp.float32),
            pltpu.VMEM(slabs, jnp.bfloat16),
            pltpu.VMEM(slabs, jnp.bfloat16),
            pltpu.VMEM(slabs, jnp.bfloat16),
            dma((steps,)), dma((n_col // 2,)), dma((n_col // 2,)),
            dma((n_col // 2,)), dma((n_col // 2,)),
            dma((steps, n_row)), dma((steps, n_row)), dma((steps, n_row)),
        ],
        compiler_params=pltpu.CompilerParams(
            collective_id=0, has_side_effects=True, vmem_limit_bytes=62 * 1024 * 1024
        ),
    )(counts, tile_values, tile_rows, tile_cols, features, weight, bias.reshape(1, width))


def solution(mesh):
    in_specs = (
        P(("groups", "row"), "col", None),
        P(("groups", "row"), "col", None, None),
        P(("groups", "row"), "col", None),
        P(("groups", "row"), "col", None),
        P(("groups", "row"), "col"),
        P(),
        P(),
    )
    out_specs = P(("groups", "col"), "row", None)
    return jax.shard_map(
        on_device, mesh=mesh, in_specs=in_specs, out_specs=out_specs, check_vma=False
    )
```

```python
import functools

import jax
import jax.numpy as jnp
from jax import lax
from jax.experimental import pallas as pl
from jax.experimental.pallas import tpu as pltpu
from jax.sharding import PartitionSpec as P

TILE = 64
LANES = 128
MESH = pl.DeviceIdType.MESH


def layer_kernel(
    n_row, n_col, live_ref, vals_hbm, rows_ref, cols_ref, feat_ref, weight_ref, bias_ref,
    out_ref, vals, pick, dense, src, swapped, acc, sent, up_in, down_in,
    vals_sem, far_send, far_recv, near_send, near_recv, send_sem, up_sem, down_sem,
):
    steps, slots, lanes = vals.shape
    cuts = far_send.shape[1]
    tiles_in = pick.shape[0]
    piece_rows = feat_ref.shape[1]
    col_tiles = src.shape[0] // TILE
    row_tiles = tiles_in // col_tiles
    half = tiles_in // 2
    chunk = min(half, 512)
    pairs = chunk // row_tiles
    own = row_tiles // n_row
    blocks = lanes // LANES
    chips = n_col // 2
    z = lax.axis_index("row")
    me = lax.axis_index("col")
    core = lax.rem(me, 2)
    sibling = me + 1 - 2 * core

    def load(step):
        return pltpu.make_async_copy(
            vals_hbm.at[0, 0, :, pl.ds(pl.multiple_of(step * lanes, lanes), lanes)],
            vals.at[step], vals_sem.at[step],
        )

    for step in range(steps):
        load(step).start()

    cut_rows = piece_rows // cuts

    def rows_of(index, cut):
        first = pl.multiple_of(index * piece_rows + cut * cut_rows, cut_rows)
        return src.at[pl.ds(first, cut_rows)]

    def far(d, cut):
        return pltpu.make_async_remote_copy(
            src_ref=feat_ref.at[0, pl.ds(cut * cut_rows, cut_rows)], dst_ref=rows_of(me, cut),
            send_sem=far_send.at[d, cut], recv_sem=far_recv.at[d, cut],
            device_id={"col": lax.rem(me + 2 * d, n_col)}, device_id_type=MESH,
        )

    def near(d, cut):
        origin = lax.rem(me + n_col - 2 * d, n_col)
        mine = feat_ref.at[0, pl.ds(cut * cut_rows, cut_rows)]
        return pltpu.make_async_remote_copy(
            src_ref=mine if d == 0 else rows_of(origin, cut), dst_ref=rows_of(origin, cut),
            send_sem=near_send.at[d, cut], recv_sem=near_recv.at[d, cut],
            device_id={"col": sibling}, device_id_type=MESH,
        )

    def passed(p, o, to, sem):
        landing = up_in if sem is up_sem else down_in
        return pltpu.make_async_remote_copy(
            src_ref=sent.at[p, o], dst_ref=landing.at[p, o],
            send_sem=send_sem.at[p, o], recv_sem=sem.at[p, o],
            device_id={"row": to}, device_id_type=MESH,
        )

    barrier = pltpu.get_barrier_semaphore()
    for d in range(1, chips):
        pl.semaphore_signal(
            barrier, inc=1, device_id={"col": lax.rem(me + 2 * d, n_col)}, device_id_type=MESH
        )
    pl.semaphore_signal(barrier, inc=1, device_id={"col": sibling}, device_id_type=MESH)

    @pl.when(z > 0)
    def _():
        pl.semaphore_signal(barrier, inc=1, device_id={"row": z - 1}, device_id_type=MESH)

    @pl.when(z < n_row - 1)
    def _():
        pl.semaphore_signal(barrier, inc=1, device_id={"row": z + 1}, device_id_type=MESH)

    beside = lax.div(z + n_row - 1, n_row) + lax.div(2 * n_row - 2 - z, n_row)
    pl.semaphore_wait(barrier, chips + beside)

    for d in range(1, chips):
        for cut in range(cuts):
            far(d, cut).start()
    for cut in range(cuts):
        near(0, cut).start()
    src[pl.ds(pl.multiple_of(me * piece_rows, piece_rows), piece_rows), :] = feat_ref[0]

    slot = lax.broadcasted_iota(jnp.int32, (1, slots), 1)
    place = (cols_ref[0] & 1) * half + (cols_ref[0] >> 1) * row_tiles + rows_ref[0]
    place = jnp.where(slot < live_ref[0, 0], place, -1)

    @pl.loop(0, tiles_in // 128)
    def _(at):
        first = pl.multiple_of(at * 128, 128)
        index = first + lax.broadcasted_iota(jnp.int32, (128, slots), 0)
        pick[pl.ds(first, 128), :] = jnp.where(index == place, 1.0, 0.0).astype(jnp.bfloat16)

    is_low = lax.broadcasted_iota(jnp.int32, (row_tiles, LANES), 1) < TILE

    def densify(step):
        def one_chunk(at, carry):
            first = pl.multiple_of(at * chunk, chunk)
            for sub in range(lanes // 256):
                block_vals = vals[step, :, sub * 256 : (sub + 1) * 256]
                even = jnp.dot(
                    pick[pl.ds(first, chunk), :], block_vals,
                    preferred_element_type=jnp.float32,
                )
                odd = jnp.dot(
                    pick[pl.ds(half + first, chunk), :], block_vals,
                    preferred_element_type=jnp.float32,
                )
                for part in range(2):
                    block = 2 * sub + part
                    cut = slice(part * LANES, (part + 1) * LANES)
                    for pair in range(pairs):
                        down = slice(pair * row_tiles, (pair + 1) * row_tiles)
                        held = even[down, cut]
                        turned = pltpu.roll(odd[down, cut], TILE, 1)
                        lane = pl.multiple_of((at * pairs + pair) * LANES, LANES)
                        where = pl.ds(block * row_tiles, row_tiles), pl.ds(lane, LANES)
                        dense[(0,) + where] = jnp.where(is_low, held, turned).astype(jnp.bfloat16)
                        dense[(1,) + where] = jnp.where(is_low, turned, held).astype(jnp.bfloat16)
            return carry

        if half == chunk:
            one_chunk(0, 0)
        else:
            lax.fori_loop(0, half // chunk, one_chunk, 0)

    def finish_gather():
        for d in range(1, chips):
            for cut in range(cuts):
                far(d, cut).wait_recv()
                near(d, cut).start()
        for d in range(chips):
            for cut in range(cuts):
                near(d, cut).wait_recv()
        for pair in range(col_tiles // 2):
            low = 2 * pair * TILE
            swapped[low : low + TILE, :] = src[low + TILE : low + 2 * TILE, :]
            swapped[low + TILE : low + 2 * TILE, :] = src[low : low + TILE, :]

    def multiply(step):
        for parity, source in ((0, src), (1, swapped)):
            sums = jnp.dot(dense[parity], source[...], preferred_element_type=jnp.float32)
            for block in range(blocks):
                for owner in range(n_row):
                    low = block * row_tiles + owner * own
                    to = (2 * block + parity) * own
                    acc[step, owner, to : to + own, :] = sums[low : low + own, :]

    def pass_on(p, is_first, sem, landing, to, owner_of, begin, end):
        def one(j, carry):
            o = owner_of(j)

            @pl.when(is_first)
            def _():
                sent[p, o] = acc[p, o].astype(jnp.bfloat16)

            @pl.when(jnp.logical_not(is_first))
            def _():
                passed(p, o, to, sem).wait_recv()
                sent[p, o] = (acc[p, o] + landing[p, o].astype(jnp.float32)).astype(jnp.bfloat16)

            passed(p, o, to, sem).start()
            return carry

        lax.fori_loop(begin, end, one, 0)

    above_count = n_row - 1 - z
    below_count = z
    above_early = jnp.minimum(above_count, jnp.maximum(above_count - 1, 1))
    below_early = jnp.minimum(below_count, jnp.maximum(below_count - 1, 1))

    def pass_up(p, begin, end):
        pass_on(p, z == 0, up_sem, up_in, z + 1, lambda j: n_row - 1 - j, begin, end)

    def pass_down(p, begin, end):
        pass_on(p, z == n_row - 1, down_sem, down_in, z - 1, lambda j: j, begin, end)

    def one_step(t, carry):
        @pl.when(t < steps)
        def _():
            load(t).wait()
            densify(t)

            @pl.when(t == 0)
            def _():
                finish_gather()

            multiply(t)

        up = t - z

        @pl.when(jnp.logical_and(up >= 0, up < steps))
        def _():
            pass_up(up, 0, above_early)

        below = t - (n_row - 1 - z)

        @pl.when(jnp.logical_and(below >= 0, below < steps))
        def _():
            pass_down(below, 0, below_early)

        return carry

    lax.fori_loop(0, steps + n_row - 1, one_step, 0)

    def late(p, carry):
        pass_up(p, above_early, above_count)
        pass_down(p, below_early, below_count)
        return carry

    lax.fori_loop(0, steps, late, 0)

    def collect(p, carry):
        @pl.when(z > 0)
        def _():
            passed(p, z, z + 1, up_sem).wait_recv()
            acc[p, z] = acc[p, z] + up_in[p, z].astype(jnp.float32)

        @pl.when(z < n_row - 1)
        def _():
            passed(p, z, z - 1, down_sem).wait_recv()
            acc[p, z] = acc[p, z] + down_in[p, z].astype(jnp.float32)

        return carry

    lax.fori_loop(0, steps, collect, 0)

    hidden = jnp.concatenate([acc[p, z].astype(jnp.bfloat16) for p in range(steps)], axis=0)
    target = lax.broadcasted_iota(jnp.int32, (piece_rows, piece_rows), 0)
    origin = lax.broadcasted_iota(jnp.int32, (piece_rows, piece_rows), 1)
    wanted = (target & (TILE - 1)) * own + (target >> 6)
    order = jnp.where(origin == wanted, 1.0, 0.0).astype(jnp.bfloat16)
    hidden = jnp.dot(order, hidden, preferred_element_type=jnp.float32).astype(jnp.bfloat16)
    mixed = jnp.dot(hidden, weight_ref[...], preferred_element_type=jnp.float32) + bias_ref[...]
    out_ref[0] = jnp.maximum(mixed, 0.0).astype(jnp.bfloat16)

    for d in range(1, chips):
        for cut in range(cuts):
            far(d, cut).wait_send()
    for d in range(chips):
        for cut in range(cuts):
            near(d, cut).wait_send()

    def drain(p, carry):
        def up_one(o, inner):
            passed(p, o, z + 1, up_sem).wait_send()
            return inner

        def down_one(o, inner):
            passed(p, o, z - 1, down_sem).wait_send()
            return inner

        lax.fori_loop(z + 1, n_row, up_one, 0)
        lax.fori_loop(0, z, down_one, 0)
        return carry

    lax.fori_loop(0, steps, drain, 0)


def on_device(features, tile_values, tile_rows, tile_cols, counts, weight, bias):
    n_row, n_col = lax.axis_size("row"), lax.axis_size("col")
    piece_rows, width = features.shape[1:]
    slots, entries = tile_values.shape[2:]
    own = piece_rows // TILE
    row_tiles = n_row * own
    source_rows = n_col * piece_rows
    tiles_in = row_tiles * source_rows // TILE
    steps = 2 if tiles_in <= 2048 else 8
    lanes = entries // steps
    blocks = lanes // LANES
    part_rows = 2 * blocks * own
    vmem = pl.BlockSpec(memory_space=pltpu.VMEM)
    slabs = (steps, n_row, part_rows, width)
    dma = pltpu.SemaphoreType.DMA
    return pl.pallas_call(
        functools.partial(layer_kernel, n_row, n_col),
        in_specs=[
            pl.BlockSpec(memory_space=pltpu.SMEM), pl.BlockSpec(memory_space=pl.ANY),
            vmem, vmem, vmem, vmem, vmem,
        ],
        out_specs=vmem,
        out_shape=jax.ShapeDtypeStruct((1, piece_rows, width), jnp.bfloat16),
        scratch_shapes=[
            pltpu.VMEM((steps, slots, lanes), jnp.bfloat16),
            pltpu.VMEM((tiles_in, slots), jnp.bfloat16),
            pltpu.VMEM((2, blocks * row_tiles, source_rows), jnp.bfloat16),
            pltpu.VMEM((source_rows, width), jnp.bfloat16),
            pltpu.VMEM((source_rows, width), jnp.bfloat16),
            pltpu.VMEM(slabs, jnp.float32),
            pltpu.VMEM(slabs, jnp.bfloat16),
            pltpu.VMEM(slabs, jnp.bfloat16),
            pltpu.VMEM(slabs, jnp.bfloat16),
            dma((steps,)), dma((n_col // 2, 4)), dma((n_col // 2, 4)),
            dma((n_col // 2, 4)), dma((n_col // 2, 4)),
            dma((steps, n_row)), dma((steps, n_row)), dma((steps, n_row)),
        ],
        compiler_params=pltpu.CompilerParams(
            collective_id=0, has_side_effects=True, vmem_limit_bytes=62 * 1024 * 1024
        ),
    )(counts, tile_values, tile_rows, tile_cols, features, weight, bias.reshape(1, width))


def solution(mesh):
    in_specs = (
        P(("groups", "row"), "col", None),
        P(("groups", "row"), "col", None, None),
        P(("groups", "row"), "col", None),
        P(("groups", "row"), "col", None),
        P(("groups", "row"), "col"),
        P(),
        P(),
    )
    out_specs = P(("groups", "col"), "row", None)
    return jax.shard_map(
        on_device, mesh=mesh, in_specs=in_specs, out_specs=out_specs, check_vma=False
    )
```
